32 devices in a mesh: blk: 4 (over x, core), wide: 8 (over z, y).
Axes of the slice: x: 2, y: 2, z: 4, core: 2. Of those that a mesh axis runs over, the one named last changes fastest.
Arguments:
- patch_keys: float32 [32, 196, 512], P(('blk', 'wide')), may hold values from -16 to 16
- patch_values: float32 [32, 196, 512], P(('blk', 'wide')), may hold values from -6 to 6
- caption_queries: float32 [32, 512], P(('blk', 'wide')), may hold values from -48 to 48
- positive: int32 [32, 32], P(('blk', 'wide')), may hold values 0 or 1
Outputs:
- grad_keys: float32 [32, 196, 512], P(('blk', 'wide'))
- grad_values: float32 [32, 196, 512], P(('blk', 'wide'))
- grad_queries: float32 [32, 512], P(('blk', 'wide'))
The draws below stay inside these ranges and needn't reach their ends.
All inputs are finite; a program needn't handle non-finite values. No bound on the sum of `positive` on one device may be relied on, other than what follows from the above.
Results may differ from the reference program's by a relative error of at most 0.0005.
Values sent between devices are 32-bit elements; how exact they have to be, the bound alone decides.
A program may use at most 64 MiB of HBM per device.

```python
import jax
import jax.numpy as jnp
from jax import lax

D = 512
HEADS = 8
PATCHES = 196
IMAGES = 32
CAPTIONS = 32


def draw_patch_keys(key, part):
    shape = (IMAGES, PATCHES, D)
    base = jax.random.truncated_normal(jax.random.fold_in(key, 11), -5.0, 5.0, shape, jnp.float32)
    return base


def draw_caption_queries(key, part):
    shape = (CAPTIONS, D)
    scales = jnp.exp(jax.random.uniform(jax.random.fold_in(key, 13), (CAPTIONS, 1), jnp.float32, jnp.log(0.3), jnp.log(3.0)))
    base = jax.random.truncated_normal(jax.random.fold_in(key, 17), -5.0, 5.0, shape, jnp.float32) * scales
    return base


def plant(entries, own_key, least, largest):
    spot = [jax.random.randint(jax.random.fold_in(own_key, axis), (), 0, length) for axis, length in enumerate(entries.shape)]
    widest = entries.shape.index(max(entries.shape))
    neighbour = spot[:widest] + [(spot[widest] + 1) % entries.shape[widest]] + spot[widest + 1:]
    return entries.at[tuple(spot)].set(least).at[tuple(neighbour)].set(largest)


def level_of(stream_key, extent, split, smallest, high):
    def one(axis_at, blocks):
        heights = jax.random.uniform(jax.random.fold_in(jax.random.fold_in(stream_key, 6), axis_at), (blocks,), jnp.float32, smallest / len(split), high / len(split))
        return jnp.repeat(jnp.exp(heights), extent[axis_at] // blocks).reshape((-1,) + (1,) * (len(extent) - axis_at - 1))

    level = one(*split[0])
    for cut in split[1:]:
        level = level * one(*cut)
    return level


def noise(own_key, extent, scale, bound, cuts=(), dtype=jnp.bfloat16):
    values = jax.random.normal(own_key, extent, jnp.float32) * scale
    if len(cuts) > 0:
        values = level_of(own_key, extent, cuts, -0.22, 0.18) * values
    return jnp.clip(values, min=-bound, max=bound).astype(dtype)


def setup_inputs(seed: int = 0) -> dict:
    key_of = jax.random.split(jax.random.key(seed), 5)
    patch_keys = draw_patch_keys(jax.random.fold_in(key_of[4], 71), 0)
    patch_values = noise(key_of[1], (IMAGES, PATCHES, D), 1.0, 6.0, ((0, 32),), jnp.float32)
    caption_queries = draw_caption_queries(jax.random.fold_in(key_of[4], 71), 0)
    positive = plant((jax.random.randint(key_of[3], (IMAGES, CAPTIONS), 0, 128) < 1).astype(jnp.int32), jax.random.fold_in(key_of[3], 1), 0, 1)
    return dict(patch_keys=patch_keys, patch_values=patch_values, caption_queries=caption_queries, positive=positive)


epsilon = 1e-06
similarity_multiplier = 10.0
similarity_shift_term = -2.0

def pair_loss(keys, values, queries, labels):
    images, patches, width = keys.shape
    row_count = queries.shape[0]
    head_dim = width // HEADS
    query_heads = queries.reshape(row_count, HEADS, head_dim)
    key_heads = keys.reshape(images, patches, HEADS, head_dim)
    value_heads = values.reshape(images, patches, HEADS, head_dim)
    scores = jnp.einsum('chd,iphd->ichp', query_heads, key_heads, precision=lax.Precision.HIGHEST) * head_dim ** (-0.5)
    row_max = lax.stop_gradient(lax.optimization_barrier(jnp.max(scores, axis=3, keepdims=True)))
    exponent = jnp.exp(scores - row_max)
    weights = exponent / lax.optimization_barrier(jnp.sum(exponent, axis=3, keepdims=True))
    pooled = jnp.einsum('ichp,iphd->ichd', weights, value_heads, precision=lax.Precision.HIGHEST).reshape(images, row_count, width)
    matching_similarity = lax.optimization_barrier(jnp.mean(pooled * queries[None], axis=2))
    summary_reciprocal_length = lax.rsqrt(lax.optimization_barrier(jnp.mean(pooled * pooled, axis=2)) + epsilon)
    probe_reciprocal_length = lax.rsqrt(lax.optimization_barrier(jnp.mean(queries * queries, axis=1)) + epsilon)
    matching_scaled_scores = similarity_multiplier * matching_similarity * summary_reciprocal_length * probe_reciprocal_length[None] + similarity_shift_term
    label_signs = 2.0 * labels.astype(jnp.float32) - 1.0
    return jnp.sum(jnp.logaddexp(0.0, -label_signs * matching_scaled_scores))

def reference(patch_keys, patch_values, caption_queries, positive):

    def image_step(query_total, packed):
        one_keys, one_values, one_labels = packed

        def loss_of(keys_in, values_in, input_queries):
            return pair_loss(keys_in[None], values_in[None], input_queries, one_labels[None])
        total, pull_back = jax.vjp(loss_of, one_keys, one_values, caption_queries)
        key_part, value_part, query_part = pull_back(jnp.ones_like(total))
        return (query_total + query_part, (key_part, value_part))
    query_total, (grad_keys, grad_values) = lax.scan(image_step, jnp.zeros_like(caption_queries), (patch_keys, patch_values, positive))
    return (grad_keys, grad_values, query_total)
```

```python
import functools

import jax
import jax.numpy as jnp
from jax import lax
from jax.experimental import pallas as pl
from jax.experimental.pallas import tpu as pltpu
from jax.sharding import PartitionSpec as P

HEADS = 8
GROUP = 256
LANES = 128

epsilon = 1e-06
similarity_multiplier = 10.0
similarity_shift_term = -2.0

MESH = pl.DeviceIdType.MESH
F32 = jnp.float32
BF16 = jnp.bfloat16


def split(x):
    high = x.astype(BF16)
    return high, (x - high.astype(F32)).astype(BF16)


def dot3(a, b, dims):
    def one(x, y):
        return lax.dot_general(x, y, (dims, ((), ())), preferred_element_type=F32)

    return one(a[0], b[0]) + (one(a[0], b[1]) + one(a[1], b[0]))


NN = ((1,), (0,))
NT = ((1,), (1,))
TN = ((0,), (0,))


def remote(src, dst, send, recv, where):
    return pltpu.make_async_remote_copy(
        src_ref=src, dst_ref=dst, send_sem=send, recv_sem=recv,
        device_id=where, device_id_type=MESH,
    )


def kernel(
    nblk, nwide, block,
    k_hbm, v_hbm, q_ref, pos_ref,
    dk_hbm, dv_hbm, dq_ref,
    k_in, v_in, khi, klo, vhi, vlo, dk_buf, dv_buf,
    gath, part, land1, acc, land2,
    load_sem, store_sem,
    g1s, g1r, g2s, g2r, r1s, r1r, r2s, r2r,
):
    padded, width = khi.shape
    pieces = width // LANES
    patches = k_hbm.shape[0] // pieces
    rows = gath.shape[0]
    groups = width // GROUP
    head_dim = width // HEADS
    per_group = GROUP // head_dim
    scale = head_dim ** (-0.5)
    me_b = lax.axis_index("blk")
    me_w = lax.axis_index("wide")
    me = me_b * nwide + me_w

    k_load = pltpu.make_async_copy(k_hbm, k_in, load_sem.at[0])
    v_load = pltpu.make_async_copy(v_hbm, v_in, load_sem.at[1])
    k_load.start()
    v_load.start()

    wide_peers = [lax.rem(me_w + s, nwide) for s in range(1, nwide)]
    blk_peers = [lax.rem(me_b + s, nblk) for s in range(1, nblk)]

    barrier = pltpu.get_barrier_semaphore()
    for w in wide_peers:
        pl.semaphore_signal(barrier, inc=1, device_id=(me_b, w), device_id_type=MESH)
    for b in blk_peers:
        pl.semaphore_signal(barrier, inc=1, device_id=(b, me_w), device_id_type=MESH)

    gath[pl.ds(me, 1), :] = q_ref[...]
    pl.semaphore_wait(barrier, nblk + nwide - 2)

    mine = gath.at[pl.ds(me, 1)]
    sends1 = []
    for s, w in enumerate(wide_peers):
        copy = remote(q_ref, mine, g1s.at[s], g1r.at[s], (me_b, w))
        copy.start()
        sends1.append(copy)

    def prepare(load, raw, high, low):
        load.wait()
        if padded > patches:
            tail = patches // 16 * 16
            high[tail:, :] = jnp.zeros((padded - tail, width), BF16)
            low[tail:, :] = jnp.zeros((padded - tail, width), BF16)
        for g in range(pieces):
            h, l = split(raw[pl.ds(g, patches, stride=pieces), :])
            high[:patches, g * LANES:(g + 1) * LANES] = h
            low[:patches, g * LANES:(g + 1) * LANES] = l

    prepare(k_load, k_in, khi, klo)

    for copy in sends1:
        copy.wait_recv()
    own = gath.at[pl.ds(pl.multiple_of(me_b * nwide, nwide), nwide)]
    sends2 = []
    for s, b in enumerate(blk_peers):
        copy = remote(own, own, g2s.at[s], g2r.at[s], (b, me_w))
        copy.start()
        sends2.append(copy)

    prepare(v_load, v_in, vhi, vlo)

    for copy in sends2:
        copy.wait_recv()

    stacked = per_group * block
    row = lax.broadcasted_iota(jnp.int32, (stacked, GROUP), 0) // block
    col = lax.broadcasted_iota(jnp.int32, (stacked, GROUP), 1) // head_dim
    on_head = row == col
    valid = lax.broadcasted_iota(jnp.int32, (stacked, padded), 1) < patches

    def spread(x):
        return jnp.where(on_head, jnp.concatenate([x] * per_group, axis=0), 0.0)

    def gathered(x):
        x = jnp.where(on_head, x, 0.0)
        return sum(x[h * block:(h + 1) * block] for h in range(per_group))

    def cut(ref, j):
        return ref[:, j * GROUP:(j + 1) * GROUP]

    def chunk(at):
        q = gath[pl.ds(at, block), :]
        pos = pos_ref[at // block]
        eye = lax.broadcasted_iota(jnp.int32, (block, block), 0) == lax.broadcasted_iota(
            jnp.int32, (block, block), 1
        )
        label = jnp.sum(jnp.where(eye, pos.astype(F32), 0.0), axis=1, keepdims=True)
        sign = 2.0 * label - 1.0
        q_mean = jnp.mean(q * q, axis=1, keepdims=True)
        qg = [q[:, j * GROUP:(j + 1) * GROUP] for j in range(groups)]
        qbd = [split(spread(x * scale)) for x in qg]

        e, e2, rinv, pooled = [], [], [], []
        for j in range(groups):
            s = dot3(qbd[j], (cut(khi, j), cut(klo, j)), NT)
            s = jnp.where(valid, s, -3e38)
            x = jnp.exp(s - jnp.max(s, axis=1, keepdims=True))
            e.append(x)
            e2.append(split(x))
            rinv.append(1.0 / jnp.sum(x, axis=1, keepdims=True))
            y = dot3(e2[j], (cut(vhi, j), cut(vlo, j)), NN)
            pooled.append(gathered(y * rinv[j]))

        a = sum(jnp.sum(p * x, axis=1, keepdims=True) for p, x in zip(pooled, qg)) / width
        b = sum(jnp.sum(p * p, axis=1, keepdims=True) for p in pooled) / width
        r = lax.rsqrt(b + epsilon)
        u = lax.rsqrt(q_mean + epsilon)
        logit = similarity_multiplier * a * r * u + similarity_shift_term
        g = -sign / (1.0 + jnp.exp(sign * logit))
        t = g * (similarity_multiplier / width) * r * u
        ar = t * a * r * r
        au = t * a * u * u

        ds2, dpbd = [], []
        for j in range(groups):
            dp = t * qg[j] - ar * pooled[j]
            full = spread(dp) * rinv[j]
            pd = jnp.concatenate([pooled[j]] * per_group, axis=0)
            rs = jnp.sum(full * pd, axis=1, keepdims=True)
            dpbd.append(split(full))
            dw = dot3(dpbd[j], (cut(vhi, j), cut(vlo, j)), NT)
            ds = e[j] * (dw - rs)
            ds2.append(split(ds))
            dq = gathered(dot3(ds2[j], (cut(khi, j), cut(klo, j)), NN)) * scale
            part[pl.ds(at, block), j * GROUP:(j + 1) * GROUP] = dq + (t * pooled[j] - au * qg[j])
        return qbd, e2, ds2, dpbd

    def finish(state, add):
        qbd, e2, ds2, dpbd = state
        for j in range(groups):
            dk = dot3(ds2[j], qbd[j], TN)[:patches]
            dv = dot3(e2[j], dpbd[j], TN)[:patches]
            for i in range(GROUP // LANES):
                lines = pl.ds(j * (GROUP // LANES) + i, patches, stride=pieces)
                lanes = slice(i * LANES, (i + 1) * LANES)
                if add:
                    dk_buf[lines, :] += dk[:, lanes]
                    dv_buf[lines, :] += dv[:, lanes]
                else:
                    dk_buf[lines, :] = dk[:, lanes]
                    dv_buf[lines, :] = dv[:, lanes]

    one = rows == block
    if one:
        state = chunk(0)
    else:
        dk_buf[...] = jnp.zeros_like(dk_buf)
        dv_buf[...] = jnp.zeros_like(dv_buf)

        def step(i, carry):
            finish(chunk(pl.multiple_of(i * block, block)), True)
            return carry

        lax.fori_loop(0, rows // block, step, 0)

    sends3 = []
    for s, b in enumerate(blk_peers):
        copy = remote(
            part.at[pl.ds(pl.multiple_of(b * nwide, nwide), nwide)],
            land1.at[s], r1s.at[s], r1r.at[s], (b, me_w),
        )
        copy.start()
        sends3.append(copy)

    if one:
        finish(state, False)
    dk_store = pltpu.make_async_copy(dk_buf, dk_hbm, store_sem.at[0])
    dv_store = pltpu.make_async_copy(dv_buf, dv_hbm, store_sem.at[1])
    dk_store.start()
    dv_store.start()

    total = part[pl.ds(pl.multiple_of(me_b * nwide, nwide), nwide), :]
    for s, copy in enumerate(sends3):
        copy.wait_recv()
        total = total + land1[s]
    acc[...] = total

    sends4 = []
    for s, w in enumerate(wide_peers):
        copy = remote(
            acc.at[pl.ds(w, 1)], land2.at[pl.ds(s, 1)], r2s.at[s], r2r.at[s], (me_b, w)
        )
        copy.start()
        sends4.append(copy)
    final = acc[pl.ds(me_w, 1), :]
    for copy in sends4:
        copy.wait_recv()
    final = final + jnp.sum(land2[:nwide - 1, :], axis=0, keepdims=True)
    dq_ref[...] = final

    for copy in sends1 + sends2 + sends3 + sends4:
        copy.wait_send()
    dk_store.wait()
    dv_store.wait()


def per_device(nblk, nwide, patch_keys, patch_values, caption_queries, positive):
    _, patches, width = patch_keys.shape
    rows = positive.shape[1]
    padded = -(-patches // LANES) * LANES
    block = 32 if rows % 32 == 0 else rows
    lines = patches * width // LANES
    flat = (lines, LANES)
    any_space = pl.BlockSpec(memory_space=pltpu.HBM)
    vmem = pl.BlockSpec(memory_space=pltpu.VMEM)
    dma = pltpu.SemaphoreType.DMA
    dk, dv, dq = pl.pallas_call(
        functools.partial(kernel, nblk, nwide, block),
        out_shape=(
            jax.ShapeDtypeStruct(flat, F32),
            jax.ShapeDtypeStruct(flat, F32),
            jax.ShapeDtypeStruct(caption_queries.shape, F32),
        ),
        in_specs=[any_space, any_space, vmem, vmem],
        out_specs=(any_space, any_space, vmem),
        scratch_shapes=[
            pltpu.VMEM(flat, F32),
            pltpu.VMEM(flat, F32),
            pltpu.VMEM((padded, width), BF16),
            pltpu.VMEM((padded, width), BF16),
            pltpu.VMEM((padded, width), BF16),
            pltpu.VMEM((padded, width), BF16),
            pltpu.VMEM(flat, F32),
            pltpu.VMEM(flat, F32),
            pltpu.VMEM((rows, width), F32),
            pltpu.VMEM((rows, width), F32),
            pltpu.VMEM((nblk - 1, nwide, width), F32),
            pltpu.VMEM((nwide, width), F32),
            pltpu.VMEM((nwide, width), F32),
            dma((2,)),
            dma((2,)),
            dma((nwide - 1,)), dma((nwide - 1,)),
            dma((nblk - 1,)), dma((nblk - 1,)),
            dma((nblk - 1,)), dma((nblk - 1,)),
            dma((nwide - 1,)), dma((nwide - 1,)),
        ],
        compiler_params=pltpu.CompilerParams(
            collective_id=0, has_side_effects=True, vmem_limit_bytes=60 * 1024 * 1024
        ),
        cost_estimate=pl.CostEstimate(
            flops=6 * 2 * 3 * rows * patches * width,
            bytes_accessed=4 * 4 * patches * width,
            transcendentals=rows * HEADS * patches,
        ),
    )(
        patch_keys.reshape(flat),
        patch_values.reshape(flat),
        caption_queries,
        positive.reshape(rows // block, 1, block),
    )
    return dk.reshape(patch_keys.shape), dv.reshape(patch_values.shape), dq


def solution(mesh):
    in_specs = (
        P(("blk", "wide"), None, None),
        P(("blk", "wide"), None, None),
        P(("blk", "wide"), None),
        P(("blk", "wide"), None),
    )
    out_specs = (
        P(("blk", "wide"), None, None),
        P(("blk", "wide"), None, None),
        P(("blk", "wide"), None),
    )
    body = functools.partial(per_device, mesh.shape["blk"], mesh.shape["wide"])
    return jax.shard_map(body, mesh=mesh, in_specs=in_specs, out_specs=out_specs, check_vma=False)
```

```python
import functools

import jax
import jax.numpy as jnp
from jax import lax
from jax.experimental import pallas as pl
from jax.experimental.pallas import tpu as pltpu
from jax.sharding import PartitionSpec as P

HEADS = 8
GROUP = 256
LANES = 128

epsilon = 1e-06
similarity_multiplier = 10.0
similarity_shift_term = -2.0

MESH = pl.DeviceIdType.MESH
F32 = jnp.float32
BF16 = jnp.bfloat16


def split(x):
    high = x.astype(BF16)
    return high, (x - high.astype(F32)).astype(BF16)


def dot3(a, b, dims):
    def one(x, y):
        return lax.dot_general(x, y, (dims, ((), ())), preferred_element_type=F32)

    return one(a[0], b[0]) + (one(a[0], b[1]) + one(a[1], b[0]))


NN = ((1,), (0,))
NT = ((1,), (1,))
TN = ((0,), (0,))


def each(count, body):
    if count <= 64:
        for i in range(count):
            body(i)
    else:
        lax.fori_loop(0, count, lambda i, carry: (body(i), carry)[1], 0)


def offsets(slot, nblk, nwide):
    turn = slot // nblk
    half = (turn + 1) // 2
    odd = turn % 2
    return slot % nblk, odd * half + (1 - odd) * ((nwide - half) % nwide)


def kernel(
    nblk, nwide, block,
    k_hbm, v_hbm, q_ref, pos_ref,
    dk_buf, dv_buf, land,
    k_in, v_in, khi, klo, vhi, vlo, gath, part,
    load_sem, store_sem, gs, gr, rs_sem, rr,
):
    padded, width = khi.shape
    pieces = width // LANES
    patches = k_hbm.shape[0] // pieces
    rows = gath.shape[0]
    groups = width // GROUP
    head_dim = width // HEADS
    per_group = GROUP // head_dim
    scale = head_dim ** (-0.5)
    me_b = lax.axis_index("blk")
    me_w = lax.axis_index("wide")

    k_load = pltpu.make_async_copy(k_hbm, k_in, load_sem.at[0])
    v_load = pltpu.make_async_copy(v_hbm, v_in, load_sem.at[1])
    k_load.start()
    v_load.start()

    def ahead(slot):
        a, b = offsets(slot, nblk, nwide)
        return lax.rem(me_b + a, nblk), lax.rem(me_w + b, nwide)

    def behind(slot):
        a, b = offsets(slot, nblk, nwide)
        return lax.rem(me_b + (nblk - a), nblk), lax.rem(me_w + (nwide - b), nwide)

    def gather_copy(i):
        slot = rows - 1 - i
        return pltpu.make_async_remote_copy(
            src_ref=q_ref, dst_ref=gath.at[pl.ds(slot, 1)],
            send_sem=gs.at[i], recv_sem=gr.at[i],
            device_id=ahead(slot), device_id_type=MESH,
        )

    def scatter_copy(i):
        slot = rows - 1 - i
        return pltpu.make_async_remote_copy(
            src_ref=part.at[pl.ds(slot, 1)], dst_ref=land.at[pl.ds(slot, 1)],
            send_sem=rs_sem.at[i], recv_sem=rr.at[i],
            device_id=behind(slot), device_id_type=MESH,
        )

    barrier = pltpu.get_barrier_semaphore()
    each(rows - 1, lambda i: pl.semaphore_signal(
        barrier, inc=1, device_id=ahead(rows - 1 - i), device_id_type=MESH
    ))
    gath[0:1, :] = q_ref[...]
    pl.semaphore_wait(barrier, rows - 1)
    each(rows - 1, lambda i: gather_copy(i).start())

    def prepare(load, raw, high, low):
        load.wait()
        if padded > patches:
            tail = patches // 16 * 16
            high[tail:, :] = jnp.zeros((padded - tail, width), BF16)
            low[tail:, :] = jnp.zeros((padded - tail, width), BF16)
        for g in range(pieces):
            h, l = split(raw[pl.ds(g, patches, stride=pieces), :])
            high[:patches, g * LANES:(g + 1) * LANES] = h
            low[:patches, g * LANES:(g + 1) * LANES] = l

    prepare(k_load, k_in, khi, klo)
    prepare(v_load, v_in, vhi, vlo)
    each(rows - 1, lambda i: gather_copy(i).wait_send())
    each(rows - 1, lambda i: gather_copy(i).wait_recv())

    stacked = per_group * block
    row = lax.broadcasted_iota(jnp.int32, (stacked, GROUP), 0) // block
    col = lax.broadcasted_iota(jnp.int32, (stacked, GROUP), 1) // head_dim
    on_head = row == col
    valid = lax.broadcasted_iota(jnp.int32, (stacked, padded), 1) < patches

    def spread(x):
        return jnp.where(on_head, jnp.concatenate([x] * per_group, axis=0), 0.0)

    def gathered(x):
        x = jnp.where(on_head, x, 0.0)
        return sum(x[h * block:(h + 1) * block] for h in range(per_group))

    def cut(ref, j):
        return ref[:, j * GROUP:(j + 1) * GROUP]

    def chunk(at):
        q = gath[pl.ds(at, block), :]
        slot = at + lax.broadcasted_iota(jnp.int32, (block, 1), 0)
        a, b = offsets(slot, nblk, nwide)
        caption = (me_b + nblk - a) % nblk * nwide + (me_w + nwide - b) % nwide
        lane = lax.broadcasted_iota(jnp.int32, (block, rows), 1)
        label = jnp.sum(
            jnp.where(lane == caption, pos_ref[...].astype(F32), 0.0), axis=1, keepdims=True
        )
        sign = 2.0 * label - 1.0
        q_mean = jnp.mean(q * q, axis=1, keepdims=True)
        qg = [q[:, j * GROUP:(j + 1) * GROUP] for j in range(groups)]
        qbd = [split(spread(x * scale)) for x in qg]

        e, e2, rinv, pooled = [], [], [], []
        for j in range(groups):
            s = dot3(qbd[j], (cut(khi, j), cut(klo, j)), NT)
            s = jnp.where(valid, s, -3e38)
            x = jnp.exp(s - jnp.max(s, axis=1, keepdims=True))
            e.append(x)
            e2.append(split(x))
            rinv.append(1.0 / jnp.sum(x, axis=1, keepdims=True))
            y = dot3(e2[j], (cut(vhi, j), cut(vlo, j)), NN)
            pooled.append(gathered(y * rinv[j]))

        a = sum(jnp.sum(p * x, axis=1, keepdims=True) for p, x in zip(pooled, qg)) / width
        b = sum(jnp.sum(p * p, axis=1, keepdims=True) for p in pooled) / width
        r = lax.rsqrt(b + epsilon)
        u = lax.rsqrt(q_mean + epsilon)
        logit = similarity_multiplier * a * r * u + similarity_shift_term
        g = -sign / (1.0 + jnp.exp(sign * logit))
        t = g * (similarity_multiplier / width) * r * u
        ar = t * a * r * r
        au = t * a * u * u

        ds2, dpbd = [], []
        for j in range(groups):
            dp = t * qg[j] - ar * pooled[j]
            full = spread(dp) * rinv[j]
            pd = jnp.concatenate([pooled[j]] * per_group, axis=0)
            rs = jnp.sum(full * pd, axis=1, keepdims=True)
            dpbd.append(split(full))
            dw = dot3(dpbd[j], (cut(vhi, j), cut(vlo, j)), NT)
            ds = e[j] * (dw - rs)
            ds2.append(split(ds))
            dq = gathered(dot3(ds2[j], (cut(khi, j), cut(klo, j)), NN)) * scale
            part[pl.ds(at, block), j * GROUP:(j + 1) * GROUP] = dq + (t * pooled[j] - au * qg[j])
        return qbd, e2, ds2, dpbd

    def finish(state, add):
        qbd, e2, ds2, dpbd = state
        for j in range(groups):
            dk = dot3(ds2[j], qbd[j], TN)[:patches]
            dv = dot3(e2[j], dpbd[j], TN)[:patches]
            for i in range(GROUP // LANES):
                lines = pl.ds(j * (GROUP // LANES) + i, patches, stride=pieces)
                lanes = slice(i * LANES, (i + 1) * LANES)
                if add:
                    dk_buf[lines, :] += dk[:, lanes]
                    dv_buf[lines, :] += dv[:, lanes]
                else:
                    dk_buf[lines, :] = dk[:, lanes]
                    dv_buf[lines, :] = dv[:, lanes]

    one = rows == block
    if one:
        state = chunk(0)
    else:
        dk_buf[...] = jnp.zeros_like(dk_buf)
        dv_buf[...] = jnp.zeros_like(dv_buf)

        def step(i, carry):
            finish(chunk(pl.multiple_of(i * block, block)), True)
            return carry

        lax.fori_loop(0, rows // block, step, 0)

    each(rows - 1, lambda i: scatter_copy(i).start())
    own = pltpu.make_async_copy(part.at[0:1], land.at[0:1], store_sem.at[0])
    own.start()

    if one:
        finish(state, False)

    own.wait()
    each(rows - 1, lambda i: scatter_copy(i).wait_send())
    each(rows - 1, lambda i: scatter_copy(i).wait_recv())


def write_kernel(dk_in, dv_in, land, dk_out, dv_out, dq_ref, sems):
    dk_copy = pltpu.make_async_copy(dk_in, dk_out, sems.at[0])
    dv_copy = pltpu.make_async_copy(dv_in, dv_out, sems.at[1])
    dk_copy.start()
    dv_copy.start()
    dq_ref[...] = jnp.sum(land[...], axis=0, keepdims=True)
    dk_copy.wait()
    dv_copy.wait()


def per_device(nblk, nwide, patch_keys, patch_values, caption_queries, positive):
    _, patches, width = patch_keys.shape
    rows = positive.shape[1]
    padded = -(-patches // LANES) * LANES
    block = 32 if rows % 32 == 0 else rows
    flat = (patches * width // LANES, LANES)
    hbm = pl.BlockSpec(memory_space=pltpu.HBM)
    anywhere = pl.BlockSpec(memory_space=pl.ANY)
    vmem = pl.BlockSpec(memory_space=pltpu.VMEM)
    dma = pltpu.SemaphoreType.DMA
    big = jax.ShapeDtypeStruct(flat, F32)
    dk, dv, land = pl.pallas_call(
        functools.partial(kernel, nblk, nwide, block),
        out_shape=(pltpu.VMEM(flat, F32), pltpu.VMEM(flat, F32), pltpu.VMEM((rows, width), F32)),
        in_specs=[hbm, hbm, vmem, vmem],
        out_specs=(vmem, vmem, vmem),
        scratch_shapes=[
            pltpu.VMEM(flat, F32),
            pltpu.VMEM(flat, F32),
            pltpu.VMEM((padded, width), BF16),
            pltpu.VMEM((padded, width), BF16),
            pltpu.VMEM((padded, width), BF16),
            pltpu.VMEM((padded, width), BF16),
            pltpu.VMEM((rows, width), F32),
            pltpu.VMEM((rows, width), F32),
            dma((2,)),
            dma((1,)),
            dma((rows - 1,)), dma((rows - 1,)), dma((rows - 1,)), dma((rows - 1,)),
        ],
        compiler_params=pltpu.CompilerParams(
            collective_id=0, has_side_effects=True, vmem_limit_bytes=60 * 1024 * 1024
        ),
        cost_estimate=pl.CostEstimate(
            flops=6 * 2 * 3 * rows * patches * width,
            bytes_accessed=4 * 4 * patches * width,
            transcendentals=rows * HEADS * patches,
        ),
    )(
        patch_keys.reshape(flat),
        patch_values.reshape(flat),
        caption_queries,
        positive,
    )
    dk, dv, dq = pl.pallas_call(
        write_kernel,
        out_shape=(big, big, jax.ShapeDtypeStruct(caption_queries.shape, F32)),
        in_specs=[vmem, vmem, vmem],
        out_specs=(hbm, hbm, vmem),
        scratch_shapes=[dma((2,))],
        compiler_params=pltpu.CompilerParams(vmem_limit_bytes=4 * 1024 * 1024),
    )(dk, dv, land)
    return dk.reshape(patch_keys.shape), dv.reshape(patch_values.shape), dq


def solution(mesh):
    in_specs = (
        P(("blk", "wide"), None, None),
        P(("blk", "wide"), None, None),
        P(("blk", "wide"), None),
        P(("blk", "wide"), None),
    )
    out_specs = (
        P(("blk", "wide"), None, None),
        P(("blk", "wide"), None, None),
        P(("blk", "wide"), None),
    )
    body = functools.partial(per_device, mesh.shape["blk"], mesh.shape["wide"])
    return jax.shard_map(body, mesh=mesh, in_specs=in_specs, out_specs=out_specs, check_vma=False)
```

```python
import functools

import jax
import jax.numpy as jnp
from jax import lax
from jax.experimental import pallas as pl
from jax.experimental.pallas import tpu as pltpu
from jax.sharding import PartitionSpec as P

HEADS = 8
GROUP = 256
LANES = 128

epsilon = 1e-06
similarity_multiplier = 10.0
similarity_shift_term = -2.0

MESH = pl.DeviceIdType.MESH
F32 = jnp.float32
BF16 = jnp.bfloat16


def split(x):
    high = x.astype(BF16)
    return high, (x - high.astype(F32)).astype(BF16)


def dot3(a, b, dims):
    def one(x, y):
        return lax.dot_general(x, y, (dims, ((), ())), preferred_element_type=F32)

    return one(a[0], b[0]) + (one(a[0], b[1]) + one(a[1], b[0]))


NN = ((1,), (0,))
TN = ((0,), (0,))


def each(count, body):
    if count <= 64:
        for i in range(count):
            body(i)
    else:
        lax.fori_loop(0, count, lambda i, carry: (body(i), carry)[1], 0)


def offsets(slot, nblk, nwide):
    turn = slot // nblk
    half = (turn + 1) // 2
    odd = turn % 2
    return slot % nblk, odd * half + (1 - odd) * ((nwide - half) % nwide)


def kernel(
    nblk, nwide, block,
    k_hbm, v_hbm, q_ref, pos_ref,
    dk_buf, dv_buf, land,
    k_in, v_in, khi, klo, vhi, vlo, kht, klt, vht, vlt, gath, part,
    load_sem, store_sem, gs, gr, rs_sem, rr,
):
    padded, width = khi.shape
    pieces = width // LANES
    patches = k_hbm.shape[0] // pieces
    rows = gath.shape[0]
    groups = width // GROUP
    head_dim = width // HEADS
    per_group = GROUP // head_dim
    scale = head_dim ** (-0.5)
    me_b = lax.axis_index("blk")
    me_w = lax.axis_index("wide")

    k_load = pltpu.make_async_copy(k_hbm, k_in, load_sem.at[0])
    v_load = pltpu.make_async_copy(v_hbm, v_in, load_sem.at[1])
    k_load.start()
    v_load.start()

    def ahead(slot):
        a, b = offsets(slot, nblk, nwide)
        return lax.rem(me_b + a, nblk), lax.rem(me_w + b, nwide)

    def behind(slot):
        a, b = offsets(slot, nblk, nwide)
        return lax.rem(me_b + (nblk - a), nblk), lax.rem(me_w + (nwide - b), nwide)

    def gather_copy(i):
        slot = rows - 1 - i
        return pltpu.make_async_remote_copy(
            src_ref=q_ref, dst_ref=gath.at[pl.ds(slot, 1)],
            send_sem=gs.at[i], recv_sem=gr.at[i],
            device_id=ahead(slot), device_id_type=MESH,
        )

    def scatter_copy(i):
        slot = rows - 1 - i
        return pltpu.make_async_remote_copy(
            src_ref=part.at[pl.ds(slot, 1)], dst_ref=land.at[pl.ds(slot, 1)],
            send_sem=rs_sem.at[i], recv_sem=rr.at[i],
            device_id=behind(slot), device_id_type=MESH,
        )

    barrier = pltpu.get_barrier_semaphore()
    each(rows - 1, lambda i: pl.semaphore_signal(
        barrier, inc=1, device_id=ahead(rows - 1 - i), device_id_type=MESH
    ))
    gath[0:1, :] = q_ref[...]
    pl.semaphore_wait(barrier, rows - 1)
    each(rows - 1, lambda i: gather_copy(i).start())

    def prepare(load, raw, high, low, high_t, low_t):
        load.wait()
        if padded > patches:
            tail = patches // 16 * 16
            high[tail:, :] = jnp.zeros((padded - tail, width), BF16)
            low[tail:, :] = jnp.zeros((padded - tail, width), BF16)
        for g in range(pieces):
            h, l = split(raw[pl.ds(g, patches, stride=pieces), :])
            high[:patches, g * LANES:(g + 1) * LANES] = h
            low[:patches, g * LANES:(g + 1) * LANES] = l
        for j in range(groups):
            at = slice(j * GROUP, (j + 1) * GROUP)
            high_t[at, :] = high[:, at].T
            low_t[at, :] = low[:, at].T

    prepare(k_load, k_in, khi, klo, kht, klt)
    prepare(v_load, v_in, vhi, vlo, vht, vlt)
    each(rows - 1, lambda i: gather_copy(i).wait_send())
    each(rows - 1, lambda i: gather_copy(i).wait_recv())

    stacked = per_group * block
    row = lax.broadcasted_iota(jnp.int32, (stacked, GROUP), 0) // block
    col = lax.broadcasted_iota(jnp.int32, (stacked, GROUP), 1) // head_dim
    on_head = row == col
    valid = lax.broadcasted_iota(jnp.int32, (stacked, padded), 1) < patches

    def spread(x):
        return jnp.where(on_head, jnp.concatenate([x] * per_group, axis=0), 0.0)

    def gathered(x):
        x = jnp.where(on_head, x, 0.0)
        return sum(x[h * block:(h + 1) * block] for h in range(per_group))

    def cut(ref, j):
        return ref[:, j * GROUP:(j + 1) * GROUP]

    def cut_t(ref, j):
        return ref[j * GROUP:(j + 1) * GROUP, :]

    def chunk(at):
        q = gath[pl.ds(at, block), :]
        slot = at + lax.broadcasted_iota(jnp.int32, (block, 1), 0)
        a, b = offsets(slot, nblk, nwide)
        caption = (me_b + nblk - a) % nblk * nwide + (me_w + nwide - b) % nwide
        lane = lax.broadcasted_iota(jnp.int32, (block, rows), 1)
        label = jnp.sum(
            jnp.where(lane == caption, pos_ref[...].astype(F32), 0.0), axis=1, keepdims=True
        )
        sign = 2.0 * label - 1.0
        q_mean = jnp.mean(q * q, axis=1, keepdims=True)
        qg = [q[:, j * GROUP:(j + 1) * GROUP] for j in range(groups)]
        qbd = [split(spread(x * scale)) for x in qg]

        e, e2, rinv, pooled = [], [], [], []
        for j in range(groups):
            s = dot3(qbd[j], (cut_t(kht, j), cut_t(klt, j)), NN)
            s = jnp.where(valid, s, -3e38)
            x = jnp.exp(s - jnp.max(s, axis=1, keepdims=True))
            e.append(x)
            e2.append(split(x))
            rinv.append(1.0 / jnp.sum(x, axis=1, keepdims=True))
            y = dot3(e2[j], (cut(vhi, j), cut(vlo, j)), NN)
            pooled.append(gathered(y * rinv[j]))

        a = sum(jnp.sum(p * x, axis=1, keepdims=True) for p, x in zip(pooled, qg)) / width
        b = sum(jnp.sum(p * p, axis=1, keepdims=True) for p in pooled) / width
        r = lax.rsqrt(b + epsilon)
        u = lax.rsqrt(q_mean + epsilon)
        logit = similarity_multiplier * a * r * u + similarity_shift_term
        g = -sign / (1.0 + jnp.exp(sign * logit))
        t = g * (similarity_multiplier / width) * r * u
        ar = t * a * r * r
        au = t * a * u * u

        ds2, dpbd = [], []
        for j in range(groups):
            dp = t * qg[j] - ar * pooled[j]
            full = spread(dp) * rinv[j]
            pd = jnp.concatenate([pooled[j]] * per_group, axis=0)
            rs = jnp.sum(full * pd, axis=1, keepdims=True)
            dpbd.append(split(full))
            dw = dot3(dpbd[j], (cut_t(vht, j), cut_t(vlt, j)), NN)
            ds = e[j] * (dw - rs)
            ds2.append(split(ds))
            dq = gathered(dot3(ds2[j], (cut(khi, j), cut(klo, j)), NN)) * scale
            part[pl.ds(at, block), j * GROUP:(j + 1) * GROUP] = dq + (t * pooled[j] - au * qg[j])
        return qbd, e2, ds2, dpbd

    def finish(state, add):
        qbd, e2, ds2, dpbd = state
        for j in range(groups):
            dk = dot3(ds2[j], qbd[j], TN)[:patches]
            dv = dot3(e2[j], dpbd[j], TN)[:patches]
            for i in range(GROUP // LANES):
                lines = pl.ds(j * (GROUP // LANES) + i, patches, stride=pieces)
                lanes = slice(i * LANES, (i + 1) * LANES)
                if add:
                    dk_buf[lines, :] += dk[:, lanes]
                    dv_buf[lines, :] += dv[:, lanes]
                else:
                    dk_buf[lines, :] = dk[:, lanes]
                    dv_buf[lines, :] = dv[:, lanes]

    one = rows == block
    if one:
        state = chunk(0)
    else:
        dk_buf[...] = jnp.zeros_like(dk_buf)
        dv_buf[...] = jnp.zeros_like(dv_buf)

        def step(i, carry):
            finish(chunk(pl.multiple_of(i * block, block)), True)
            return carry

        lax.fori_loop(0, rows // block, step, 0)

    each(rows - 1, lambda i: scatter_copy(i).start())
    own = pltpu.make_async_copy(part.at[0:1], land.at[0:1], store_sem.at[0])
    own.start()

    if one:
        finish(state, False)

    own.wait()
    each(rows - 1, lambda i: scatter_copy(i).wait_send())
    each(rows - 1, lambda i: scatter_copy(i).wait_recv())


def write_kernel(dk_in, dv_in, land, dk_out, dv_out, dq_ref, sems):
    dk_copy = pltpu.make_async_copy(dk_in, dk_out, sems.at[0])
    dv_copy = pltpu.make_async_copy(dv_in, dv_out, sems.at[1])
    dk_copy.start()
    dv_copy.start()
    dq_ref[...] = jnp.sum(land[...], axis=0, keepdims=True)
    dk_copy.wait()
    dv_copy.wait()


def per_device(nblk, nwide, patch_keys, patch_values, caption_queries, positive):
    _, patches, width = patch_keys.shape
    rows = positive.shape[1]
    padded = -(-patches // LANES) * LANES
    block = 32 if rows % 32 == 0 else rows
    flat = (patches * width // LANES, LANES)
    hbm = pl.BlockSpec(memory_space=pltpu.HBM)
    anywhere = pl.BlockSpec(memory_space=pl.ANY)
    vmem = pl.BlockSpec(memory_space=pltpu.VMEM)
    dma = pltpu.SemaphoreType.DMA
    big = jax.ShapeDtypeStruct(flat, F32)
    dk, dv, land = pl.pallas_call(
        functools.partial(kernel, nblk, nwide, block),
        out_shape=(pltpu.VMEM(flat, F32), pltpu.VMEM(flat, F32), pltpu.VMEM((rows, width), F32)),
        in_specs=[hbm, hbm, vmem, vmem],
        out_specs=(vmem, vmem, vmem),
        scratch_shapes=[
            pltpu.VMEM(flat, F32),
            pltpu.VMEM(flat, F32),
            pltpu.VMEM((padded, width), BF16),
            pltpu.VMEM((padded, width), BF16),
            pltpu.VMEM((padded, width), BF16),
            pltpu.VMEM((padded, width), BF16),
            pltpu.VMEM((width, padded), BF16),
            pltpu.VMEM((width, padded), BF16),
            pltpu.VMEM((width, padded), BF16),
            pltpu.VMEM((width, padded), BF16),
            pltpu.VMEM((rows, width), F32),
            pltpu.VMEM((rows, width), F32),
            dma((2,)),
            dma((1,)),
            dma((rows - 1,)), dma((rows - 1,)), dma((rows - 1,)), dma((rows - 1,)),
        ],
        compiler_params=pltpu.CompilerParams(
            collective_id=0, has_side_effects=True, vmem_limit_bytes=60 * 1024 * 1024
        ),
        cost_estimate=pl.CostEstimate(
            flops=6 * 2 * 3 * rows * patches * width,
            bytes_accessed=4 * 4 * patches * width,
            transcendentals=rows * HEADS * patches,
        ),
    )(
        patch_keys.reshape(flat),
        patch_values.reshape(flat),
        caption_queries,
        positive,
    )
    dk, dv, dq = pl.pallas_call(
        write_kernel,
        out_shape=(big, big, jax.ShapeDtypeStruct(caption_queries.shape, F32)),
        in_specs=[vmem, vmem, vmem],
        out_specs=(hbm, hbm, vmem),
        scratch_shapes=[dma((2,))],
        compiler_params=pltpu.CompilerParams(vmem_limit_bytes=4 * 1024 * 1024),
    )(dk, dv, land)
    return dk.reshape(patch_keys.shape), dv.reshape(patch_values.shape), dq


def solution(mesh):
    in_specs = (
        P(("blk", "wide"), None, None),
        P(("blk", "wide"), None, None),
        P(("blk", "wide"), None),
        P(("blk", "wide"), None),
    )
    out_specs = (
        P(("blk", "wide"), None, None),
        P(("blk", "wide"), None, None),
        P(("blk", "wide"), None),
    )
    body = functools.partial(per_device, mesh.shape["blk"], mesh.shape["wide"])
    return jax.shard_map(body, mesh=mesh, in_specs=in_specs, out_specs=out_specs, check_vma=False)
```

```python
import functools

import jax
import jax.numpy as jnp
from jax import lax
from jax.experimental import pallas as pl
from jax.experimental.pallas import tpu as pltpu
from jax.sharding import PartitionSpec as P

HEADS = 8
GROUP = 256
LANES = 128

epsilon = 1e-06
similarity_multiplier = 10.0
similarity_shift_term = -2.0

MESH = pl.DeviceIdType.MESH
F32 = jnp.float32
BF16 = jnp.bfloat16


def split(x):
    high = x.astype(BF16)
    return high, (x - high.astype(F32)).astype(BF16)


def dot3(a, b, dims):
    def one(x, y):
        return lax.dot_general(x, y, (dims, ((), ())), preferred_element_type=F32)

    if dims == TN:
        return one(a[0], b[0]) + (one(a[0], b[1]) + one(a[1], b[0]))
    m = a[0].shape[0]
    both = one(jnp.concatenate(a, axis=0), b[0])
    return both[:m] + (both[m:] + one(a[0], b[1]))


NN = ((1,), (0,))
TN = ((0,), (0,))


def each(count, body):
    if count <= 64:
        for i in range(count):
            body(i)
    else:
        lax.fori_loop(0, count, lambda i, carry: (body(i), carry)[1], 0)


def offsets(slot, nblk, nwide):
    turn = slot // nblk
    half = (turn + 1) // 2
    odd = turn % 2
    return slot % nblk, odd * half + (1 - odd) * ((nwide - half) % nwide)


def kernel(
    nblk, nwide, block,
    k_hbm, v_hbm, q_ref, pos_ref,
    dk_buf, dv_buf, land,
    k_in, v_in, khi, klo, vhi, vlo, kht, klt, vht, vlt, gath, part,
    load_sem, store_sem, gs, gr, rs_sem, rr,
):
    padded, width = khi.shape
    pieces = width // LANES
    patches = k_hbm.shape[0] // pieces
    rows = gath.shape[0]
    groups = width // GROUP
    head_dim = width // HEADS
    per_group = GROUP // head_dim
    scale = head_dim ** (-0.5)
    me_b = lax.axis_index("blk")
    me_w = lax.axis_index("wide")

    k_load = pltpu.make_async_copy(k_hbm, k_in, load_sem.at[0])
    v_load = pltpu.make_async_copy(v_hbm, v_in, load_sem.at[1])
    k_load.start()
    v_load.start()

    def ahead(slot):
        a, b = offsets(slot, nblk, nwide)
        return lax.rem(me_b + a, nblk), lax.rem(me_w + b, nwide)

    def behind(slot):
        a, b = offsets(slot, nblk, nwide)
        return lax.rem(me_b + (nblk - a), nblk), lax.rem(me_w + (nwide - b), nwide)

    def gather_copy(i):
        slot = rows - 1 - i
        return pltpu.make_async_remote_copy(
            src_ref=q_ref, dst_ref=gath.at[pl.ds(slot, 1)],
            send_sem=gs.at[i], recv_sem=gr.at[i],
            device_id=ahead(slot), device_id_type=MESH,
        )

    def scatter_copy(i):
        slot = rows - 1 - i
        return pltpu.make_async_remote_copy(
            src_ref=part.at[pl.ds(slot, 1)], dst_ref=land.at[pl.ds(slot, 1)],
            send_sem=rs_sem.at[i], recv_sem=rr.at[i],
            device_id=behind(slot), device_id_type=MESH,
        )

    barrier = pltpu.get_barrier_semaphore()
    each(rows - 1, lambda i: pl.semaphore_signal(
        barrier, inc=1, device_id=ahead(rows - 1 - i), device_id_type=MESH
    ))
    gath[0:1, :] = q_ref[...]
    pl.semaphore_wait(barrier, rows - 1)
    each(rows - 1, lambda i: gather_copy(i).start())

    def prepare(load, raw, high, low, high_t, low_t):
        load.wait()
        if padded > patches:
            tail = patches // 16 * 16
            high[tail:, :] = jnp.zeros((padded - tail, width), BF16)
            low[tail:, :] = jnp.zeros((padded - tail, width), BF16)
        for g in range(pieces):
            h, l = split(raw[pl.ds(g, patches, stride=pieces), :])
            high[:patches, g * LANES:(g + 1) * LANES] = h
            low[:patches, g * LANES:(g + 1) * LANES] = l
        for j in range(groups):
            at = slice(j * GROUP, (j + 1) * GROUP)
            high_t[at, :] = high[:, at].T
            low_t[at, :] = low[:, at].T

    prepare(k_load, k_in, khi, klo, kht, klt)
    prepare(v_load, v_in, vhi, vlo, vht, vlt)

    stacked = per_group * block
    row = lax.broadcasted_iota(jnp.int32, (stacked, GROUP), 0) // block
    col = lax.broadcasted_iota(jnp.int32, (stacked, GROUP), 1) // head_dim
    on_head = row == col
    valid = lax.broadcasted_iota(jnp.int32, (stacked, padded), 1) < patches

    def spread(x):
        return jnp.where(on_head, jnp.concatenate([x] * per_group, axis=0), 0.0)

    def gathered(x):
        x = jnp.where(on_head, x, 0.0)
        return sum(x[h * block:(h + 1) * block] for h in range(per_group))

    def cut(ref, j):
        return ref[:, j * GROUP:(j + 1) * GROUP]

    def cut_t(ref, j):
        return ref[j * GROUP:(j + 1) * GROUP, :]

    def chunk(at):
        q = gath[pl.ds(at, block), :]
        slot = at + lax.broadcasted_iota(jnp.int32, (block, 1), 0)
        a, b = offsets(slot, nblk, nwide)
        caption = (me_b + nblk - a) % nblk * nwide + (me_w + nwide - b) % nwide
        lane = lax.broadcasted_iota(jnp.int32, (block, rows), 1)
        label = jnp.sum(
            jnp.where(lane == caption, pos_ref[...].astype(F32), 0.0), axis=1, keepdims=True
        )
        sign = 2.0 * label - 1.0
        q_mean = jnp.mean(q * q, axis=1, keepdims=True)
        qg = [q[:, j * GROUP:(j + 1) * GROUP] for j in range(groups)]
        qbd = [split(spread(x * scale)) for x in qg]

        e, e2, rinv, pooled = [], [], [], []
        for j in range(groups):
            s = dot3(qbd[j], (cut_t(kht, j), cut_t(klt, j)), NN)
            s = jnp.where(valid, s, -3e38)
            x = jnp.exp(s - jnp.max(s, axis=1, keepdims=True))
            e.append(x)
            e2.append(split(x))
            rinv.append(1.0 / jnp.sum(x, axis=1, keepdims=True))
            y = dot3(e2[j], (cut(vhi, j), cut(vlo, j)), NN)
            pooled.append(gathered(y * rinv[j]))

        a = sum(jnp.sum(p * x, axis=1, keepdims=True) for p, x in zip(pooled, qg)) / width
        b = sum(jnp.sum(p * p, axis=1, keepdims=True) for p in pooled) / width
        r = lax.rsqrt(b + epsilon)
        u = lax.rsqrt(q_mean + epsilon)
        logit = similarity_multiplier * a * r * u + similarity_shift_term
        g = -sign / (1.0 + jnp.exp(sign * logit))
        t = g * (similarity_multiplier / width) * r * u
        ar = t * a * r * r
        au = t * a * u * u

        ds2, dpbd = [], []
        for j in range(groups):
            dp = t * qg[j] - ar * pooled[j]
            full = spread(dp) * rinv[j]
            pd = jnp.concatenate([pooled[j]] * per_group, axis=0)
            rs = jnp.sum(full * pd, axis=1, keepdims=True)
            dpbd.append(split(full))
            dw = dot3(dpbd[j], (cut_t(vht, j), cut_t(vlt, j)), NN)
            ds = e[j] * (dw - rs)
            ds2.append(split(ds))
            dq = gathered(dot3(ds2[j], (cut(khi, j), cut(klo, j)), NN)) * scale
            part[pl.ds(at, block), j * GROUP:(j + 1) * GROUP] = dq + (t * pooled[j] - au * qg[j])
        return qbd, e2, ds2, dpbd

    def finish(state, add):
        qbd, e2, ds2, dpbd = state
        for j in range(groups):
            dk = dot3(ds2[j], qbd[j], TN)[:patches]
            dv = dot3(e2[j], dpbd[j], TN)[:patches]
            for i in range(GROUP // LANES):
                lines = pl.ds(j * (GROUP // LANES) + i, patches, stride=pieces)
                lanes = slice(i * LANES, (i + 1) * LANES)
                if add:
                    dk_buf[lines, :] += dk[:, lanes]
                    dv_buf[lines, :] += dv[:, lanes]
                else:
                    dk_buf[lines, :] = dk[:, lanes]
                    dv_buf[lines, :] = dv[:, lanes]

    each(rows - 1, lambda i: gather_copy(i).wait_send())
    each(rows - 1, lambda i: gather_copy(i).wait_recv())

    one = rows == block
    if one:
        state = chunk(0)
    else:
        dk_buf[...] = jnp.zeros_like(dk_buf)
        dv_buf[...] = jnp.zeros_like(dv_buf)

        def step(i, carry):
            finish(chunk(pl.multiple_of(i * block, block)), True)
            return carry

        lax.fori_loop(0, rows // block, step, 0)

    each(rows - 1, lambda i: scatter_copy(i).start())
    own = pltpu.make_async_copy(part.at[0:1], land.at[0:1], store_sem.at[0])
    own.start()

    if one:
        finish(state, False)

    own.wait()
    each(rows - 1, lambda i: scatter_copy(i).wait_send())
    each(rows - 1, lambda i: scatter_copy(i).wait_recv())


def write_kernel(dk_in, dv_in, land, dk_out, dv_out, dq_ref, sems):
    dk_copy = pltpu.make_async_copy(dk_in, dk_out, sems.at[0])
    dv_copy = pltpu.make_async_copy(dv_in, dv_out, sems.at[1])
    dk_copy.start()
    dv_copy.start()
    dq_ref[...] = jnp.sum(land[...], axis=0, keepdims=True)
    dk_copy.wait()
    dv_copy.wait()


def per_device(nblk, nwide, patch_keys, patch_values, caption_queries, positive):
    _, patches, width = patch_keys.shape
    rows = positive.shape[1]
    padded = -(-patches // LANES) * LANES
    block = 32 if rows % 32 == 0 else rows
    flat = (patches * width // LANES, LANES)
    hbm = pl.BlockSpec(memory_space=pltpu.HBM)
    anywhere = pl.BlockSpec(memory_space=pl.ANY)
    vmem = pl.BlockSpec(memory_space=pltpu.VMEM)
    dma = pltpu.SemaphoreType.DMA
    big = jax.ShapeDtypeStruct(flat, F32)
    dk, dv, land = pl.pallas_call(
        functools.partial(kernel, nblk, nwide, block),
        out_shape=(pltpu.VMEM(flat, F32), pltpu.VMEM(flat, F32), pltpu.VMEM((rows, width), F32)),
        in_specs=[hbm, hbm, vmem, vmem],
        out_specs=(vmem, vmem, vmem),
        scratch_shapes=[
            pltpu.VMEM(flat, F32),
            pltpu.VMEM(flat, F32),
            pltpu.VMEM((padded, width), BF16),
            pltpu.VMEM((padded, width), BF16),
            pltpu.VMEM((padded, width), BF16),
            pltpu.VMEM((padded, width), BF16),
            pltpu.VMEM((width, padded), BF16),
            pltpu.VMEM((width, padded), BF16),
            pltpu.VMEM((width, padded), BF16),
            pltpu.VMEM((width, padded), BF16),
            pltpu.VMEM((rows, width), F32),
            pltpu.VMEM((rows, width), F32),
            dma((2,)),
            dma((1,)),
            dma((rows - 1,)), dma((rows - 1,)), dma((rows - 1,)), dma((rows - 1,)),
        ],
        compiler_params=pltpu.CompilerParams(
            collective_id=0, has_side_effects=True, vmem_limit_bytes=60 * 1024 * 1024
        ),
        cost_estimate=pl.CostEstimate(
            flops=6 * 2 * 3 * rows * patches * width,
            bytes_accessed=4 * 4 * patches * width,
            transcendentals=rows * HEADS * patches,
        ),
    )(
        patch_keys.reshape(flat),
        patch_values.reshape(flat),
        caption_queries,
        positive,
    )
    dk, dv, dq = pl.pallas_call(
        write_kernel,
        out_shape=(big, big, jax.ShapeDtypeStruct(caption_queries.shape, F32)),
        in_specs=[vmem, vmem, vmem],
        out_specs=(hbm, hbm, vmem),
        scratch_shapes=[dma((2,))],
        compiler_params=pltpu.CompilerParams(vmem_limit_bytes=4 * 1024 * 1024),
    )(dk, dv, land)
    return dk.reshape(patch_keys.shape), dv.reshape(patch_values.shape), dq


def solution(mesh):
    in_specs = (
        P(("blk", "wide"), None, None),
        P(("blk", "wide"), None, None),
        P(("blk", "wide"), None),
        P(("blk", "wide"), None),
    )
    out_specs = (
        P(("blk", "wide"), None, None),
        P(("blk", "wide"), None, None),
        P(("blk", "wide"), None),
    )
    body = functools.partial(per_device, mesh.shape["blk"], mesh.shape["wide"])
    return jax.shard_map(body, mesh=mesh, in_specs=in_specs, out_specs=out_specs, check_vma=False)
```
